128 devices in a mesh: row: 8 (over x_hi, z), col: 16 (over y, x_lo, core).
Axes of the slice: x: 4 (x_hi: 2, x_lo: 2; x = x_hi * 2 + x_lo), y: 4, z: 4, core: 2. Of those that a mesh axis runs over, the one named last changes fastest.
Arguments:
- frozen_projection_weight: bfloat16 [16384, 16384], P('row', 'col'), may hold values from -0.046875 to 0.046875
- a_master: float32 [64, 16384], P('row', 'col'), may hold values from -6 to 6
- a_first: float32 [64, 16384], P('row', 'col'), may hold values from -4 to 4
- a_second: float32 [64, 16384], P('row', 'col'), may hold values from 0.1 to 10
- bt_master: float32 [64, 16384], P('col', 'row'), may hold values from -6 to 6
- bt_first: float32 [64, 16384], P('col', 'row'), may hold values from -4 to 4
- bt_second: float32 [64, 16384], P('col', 'row'), may hold values from 0.1 to 10
- grad_a_parts: float32 [8, 64, 16384], P('row', None, 'col'), may hold values from -6 to 6
- grad_bt_parts: float32 [16, 64, 16384], P('col', None, 'row'), may hold values from -6 to 6
Outputs:
- saved: bfloat16 [8, 16384, 2048], P(None, ('row', 'col'))
- a_new: float32 [64, 16384], P('row', 'col')
- a_first_new: float32 [64, 16384], P('row', 'col')
- a_second_new: float32 [64, 16384], P('row', 'col')
- bt_new: float32 [64, 16384], P('col', 'row')
- bt_first_new: float32 [64, 16384], P('col', 'row')
- bt_second_new: float32 [64, 16384], P('col', 'row')
The draws below stay inside these ranges and needn't reach their ends.
All inputs are finite; a program needn't handle non-finite values.
Results may differ from the reference program's by a relative error of at most 0.0004.
The reference program's roundings to bfloat16 on the way count: a program that leaves them out, or rounds other values in their place, can miss the bound.
Values may be sent and summed in bfloat16 or wider, within the bound.
No kernel may reach another device: no remote copies, remote signals or barrier semaphores. Data moves between devices by JAX's collectives and lax.ppermute only.
A program may use at most 64 MiB of HBM per device.

```python
import math
import jax
import jax.numpy as jnp
from jax import lax

D = 16384
R = 64
TP = 8
STEP = 10
N_ROW = 8
N_COL = 16


def with_spikes(array, key, source, target, blocks, factor):
    owner, partner = [(jnp.arange(array.shape[axis_at]) // (array.shape[axis_at] // blocks)).reshape([-1 if axis == axis_at else 1 for axis in range(array.ndim)]) for axis_at in (source, target)]
    chosen = jax.random.permutation(key, blocks)[partner]
    strong = (owner == chosen) | (owner == (partner + blocks // 2) % blocks)
    return jnp.where(strong, factor * array, array)


def block_levels(rng, dims, pieces, least, top_value):
    loudness = 1.0
    for axis_at, shards_of in pieces:
        heights = jax.random.uniform(jax.random.fold_in(jax.random.fold_in(rng, 6), axis_at), (shards_of,), jnp.float32, least / len(pieces), top_value / len(pieces))
        loudness = loudness * jnp.repeat(jnp.exp(heights), dims[axis_at] // shards_of).reshape((-1,) + (1,) * (len(dims) - 1 - axis_at))
    return loudness


def normal_values(rng, shape, spread, bound, cuts=(), dtype=jnp.bfloat16):
    result = spread * jax.random.normal(rng, shape, jnp.float32)
    if cuts:
        result = result * block_levels(rng, shape, cuts, -0.22, 0.18)
    return jnp.clip(result, -bound, bound).astype(dtype)


def bell_draw_with(key, extent, spread, most, shards, heavy, held_as=jnp.bfloat16):
    entries = spread * jax.random.normal(key, extent, jnp.float32)
    if shards:
        entries = entries * block_levels(key, extent, shards, -0.22, 0.18)
    return jnp.clip(with_spikes(entries, jax.random.fold_in(key, 3), *heavy), -most, most).astype(held_as)


def setup_inputs(seed: int = 0) -> dict:
    arg_keys = jax.random.split(jax.random.key(seed), 10)
    return {
        "frozen_projection_weight": normal_values(arg_keys[0], (D, D), D ** -0.5, 0.046875, ((0, 8), (1, 16))),
        "a_master": normal_values(arg_keys[1], (R, D), 1.0, 6.0, ((0, 8), (1, 16)), jnp.float32),
        "a_first": normal_values(arg_keys[2], (R, D), 0.3, 4.0, ((0, 8), (1, 16)), jnp.float32),
        "a_second": jnp.clip(jnp.exp(math.log(10.0) - 4.6051702 * jax.random.uniform(arg_keys[3], (R, D), jnp.float32) ** block_levels(arg_keys[3], (R, D), ((0, 8), (1, 16)), -0.2, 0.2)), 0.1, 10.0),
        "bt_master": normal_values(arg_keys[4], (R, D), 1.0, 6.0, ((0, 16), (1, 8)), jnp.float32),
        "bt_first": normal_values(arg_keys[5], (R, D), 0.3, 4.0, ((0, 16), (1, 8)), jnp.float32),
        "bt_second": jnp.clip(jnp.exp(math.log(10.0) - 4.6051702 * jax.random.uniform(arg_keys[6], (R, D), jnp.float32) ** block_levels(arg_keys[6], (R, D), ((0, 16), (1, 8)), -0.2, 0.2)), 0.1, 10.0),
        "grad_a_parts": bell_draw_with(arg_keys[7], (N_ROW, R, D), 0.5, 6.0, ((0, 8), (2, 16)), (0, 1, 8, 2.0), jnp.float32),
        "grad_bt_parts": bell_draw_with(arg_keys[8], (N_COL, R, D), 0.5, 6.0, ((0, 16), (2, 8)), (0, 1, 16, 2.0), jnp.float32),
    }


beta_first = 0.9
beta_second = 0.95
adam_eps = 1e-08
learn_rate = 0.08

def adapter_factor():
    return 0.25 / math.sqrt(R * D)

def adam_step(master, first, second, grad):
    first_new = beta_first * first + (1.0 - beta_first) * grad
    second_new = beta_second * second + (1.0 - beta_second) * grad * grad
    corr_first = 1.0 - beta_first ** STEP
    corr_second = 1.0 - beta_second ** STEP
    update = first_new / corr_first / (jnp.sqrt(second_new / corr_second) + adam_eps)
    return (master - learn_rate * update, first_new, second_new)

def reference(frozen_projection_weight, a_master, a_first, a_second, bt_master, bt_first, bt_second, grad_a_parts, grad_bt_parts):
    grad_a = lax.optimization_barrier(jnp.sum(grad_a_parts, axis=0))
    grad_bt = lax.optimization_barrier(jnp.sum(grad_bt_parts, axis=0))
    a_new, a_first_new, a_second_new = adam_step(a_master, a_first, a_second, grad_a)
    bt_new, bt_first_new, bt_second_new = adam_step(bt_master, bt_first, bt_second, grad_bt)
    a_half = a_new.astype(jnp.bfloat16)
    bt_half = bt_new.astype(jnp.bfloat16)
    width = D // TP
    scaling = adapter_factor()
    saved_shard_paths = []
    for rank in range(TP):
        a_cols = a_half[:, rank * width:(rank + 1) * width]
        adapter_increment = jnp.dot(bt_half.T, a_cols, preferred_element_type=jnp.float32)
        frozen_column_count = frozen_projection_weight[:, rank * width:(rank + 1) * width].astype(jnp.float32)
        saved_shard_paths.append((frozen_column_count + scaling * adapter_increment).astype(jnp.bfloat16))
    saved = jnp.stack(saved_shard_paths, axis=0)
    return (saved, a_new, a_first_new, a_second_new, bt_new, bt_first_new, bt_second_new)
```

```python
import math

import jax
import jax.numpy as jnp
from jax import lax
from jax.experimental import pallas as pl
from jax.experimental.pallas import tpu as pltpu
from jax.sharding import PartitionSpec as P

D = 16384
R = 64
TP = 8
STEP = 10


beta_first = 0.9
beta_second = 0.95
adam_eps = 1e-08
learn_rate = 0.08


def adapter_factor():
    return 0.25 / math.sqrt(R * D)


def adam_step(master, first, second, grad):
    first_new = beta_first * first + (1.0 - beta_first) * grad
    second_new = beta_second * second + (1.0 - beta_second) * grad * grad
    corr_first = 1.0 - beta_first**STEP
    corr_second = 1.0 - beta_second**STEP
    update = first_new / corr_first / (jnp.sqrt(second_new / corr_second) + adam_eps)
    return (master - learn_rate * update, first_new, second_new)


def merge_kernel(bt_ref, *refs):
    *a_refs, frozen_ref, saved_ref = refs
    a_block = jnp.concatenate([ref[...].reshape(16, 1024) for ref in a_refs], axis=0)
    increment = lax.dot_general(
        bt_ref[...], a_block, (((0,), (0,)), ((), ())), preferred_element_type=jnp.float32
    )
    frozen = frozen_ref[...].reshape(128, 1024).astype(jnp.float32)
    merged = frozen + adapter_factor() * increment
    saved_ref[...] = merged.astype(jnp.bfloat16).reshape(1, 128, 1024)


def merge(bt_rows, a_parts, arrived):
    return pl.pallas_call(
        merge_kernel,
        grid=(16,),
        in_specs=[pl.BlockSpec((64, 128), lambda k: (0, 0))]
        + [pl.BlockSpec((1, 16, 1024), lambda k: (k, 0, 0))] * 4
        + [pl.BlockSpec((1, 128, 1024), lambda k: (k, 0, 0))],
        out_specs=pl.BlockSpec((1, 128, 1024), lambda k: (k // 2, 0, k % 2)),
        out_shape=jax.ShapeDtypeStruct((8, 128, 2048), jnp.bfloat16),
        cost_estimate=pl.CostEstimate(flops=2 * 128 * 64 * 16384, bytes_accessed=10 << 20, transcendentals=0),
    )(bt_rows, *a_parts, arrived)


def per_device(
    frozen_projection_weight,
    a_master,
    a_first,
    a_second,
    bt_master,
    bt_first,
    bt_second,
    grad_a_parts,
    grad_bt_parts,
):
    z = lax.axis_index("row") % 4
    arrived = lax.all_to_all(
        frozen_projection_weight.reshape(16, 128, 1024), "col", 0, 0, tiled=True
    )
    grad_a = lax.all_to_all(grad_a_parts.reshape(8, 8, 1024), "row", 0, 0, tiled=True).sum(0)
    grad_bt = lax.all_to_all(grad_bt_parts.reshape(16, 4, 2048), "col", 0, 0, tiled=True).sum(0)
    a_new, a_first_new, a_second_new = adam_step(a_master, a_first, a_second, grad_a)
    bt_new, bt_first_new, bt_second_new = adam_step(bt_master, bt_first, bt_second, grad_bt)
    a_half = a_new.astype(jnp.bfloat16)
    bt_half = bt_new.astype(jnp.bfloat16)

    low = lax.axis_index("row") < 4
    a_other = lax.ppermute(a_half, "row", [(i, i ^ 4) for i in range(8)])
    a_pair = jnp.where(low, jnp.concatenate([a_half, a_other]), jnp.concatenate([a_other, a_half]))
    a_cols = lax.all_to_all(jnp.broadcast_to(a_pair[None], (16, 16, 1024)), "col", 0, 0, tiled=True)
    a_parts = [a_cols] + [
        lax.ppermute(a_cols, "row", [(i, i // 4 * 4 + (i + k) % 4) for i in range(8)])
        for k in (1, 2, 3)
    ]
    bt_rows = lax.all_to_all(
        bt_half.reshape(4, 16, 128).transpose(1, 0, 2), "col", 0, 0, tiled=True
    ).reshape(2, 4, 8, 128)
    bt_order = jnp.concatenate(
        [
            lax.dynamic_index_in_dim(bt_rows, (z - k) % 4, 1, keepdims=False).reshape(16, 128)
            for k in range(4)
        ]
    )
    saved = merge(bt_order, a_parts, arrived)
    return (saved, a_new, a_first_new, a_second_new, bt_new, bt_first_new, bt_second_new)


def solution(mesh):
    return jax.shard_map(
        per_device,
        mesh=mesh,
        in_specs=(
            P("row", "col"),
            P("row", "col"),
            P("row", "col"),
            P("row", "col"),
            P("col", "row"),
            P("col", "row"),
            P("col", "row"),
            P("row", None, "col"),
            P("col", None, "row"),
        ),
        out_specs=(
            P(None, ("row", "col"), None),
            P("row", "col"),
            P("row", "col"),
            P("row", "col"),
            P("col", "row"),
            P("col", "row"),
            P("col", "row"),
        ),
        check_vma=False,
    )
```

```python
import math

import jax
import jax.numpy as jnp
from jax import lax
from jax.experimental import pallas as pl
from jax.experimental.pallas import tpu as pltpu
from jax.sharding import PartitionSpec as P

D = 16384
R = 64
TP = 8
STEP = 10


beta_first = 0.9
beta_second = 0.95
adam_eps = 1e-08
learn_rate = 0.08


def adapter_factor():
    return 0.25 / math.sqrt(R * D)


def adam_step(master, first, second, grad):
    first_new = beta_first * first + (1.0 - beta_first) * grad
    second_new = beta_second * second + (1.0 - beta_second) * grad * grad
    corr_first = 1.0 - beta_first**STEP
    corr_second = 1.0 - beta_second**STEP
    update = first_new / corr_first / (jnp.sqrt(second_new / corr_second) + adam_eps)
    return (master - learn_rate * update, first_new, second_new)


def mod4(value):
    return lax.rem(value + 4, 4)


def rank_order(y, x, core, x_hi, z):
    p = lax.broadcasted_iota(jnp.int32, (R, R), 0)
    s = lax.broadcasted_iota(jnp.int32, (R, R), 1)
    from_z = (z - p // 16 + 4) % 4
    from_x_hi = x_hi ^ ((p // 8) % 2)
    rank_a = 8 * (from_x_hi * 4 + from_z) + p % 8
    from_y = (y - s // 16 + 4) % 4
    from_x = x ^ ((s // 8) % 2)
    from_core = core ^ ((s // 4) % 2)
    rank_b = 4 * (from_y * 4 + from_x * 2 + from_core) + s % 4
    return (rank_a == rank_b).astype(jnp.bfloat16)


def merge_kernel(bt_ref, *refs):
    a_refs, arrived_ref, saved_ref = refs[:8], refs[8], refs[9]
    a_buf, in_buf, out_buf, a_sem, in_sem, out_sem = refs[10:]
    row, col = lax.axis_index("row"), lax.axis_index("col")
    x_hi, z = row // 4, row % 4
    y, x, core = col // 4, (col // 2) % 2, col % 2

    def source(step):
        k_core, k_y, k_x = step // 8, (step // 2) % 4, step % 2
        return mod4(y - k_y) * 4 + (x ^ k_x) * 2 + (core ^ k_core)

    a_copies = [pltpu.make_async_copy(a_refs[i], a_buf.at[i], a_sem.at[i]) for i in range(8)]
    in_copies = [
        pltpu.make_async_copy(arrived_ref.at[source(s)], in_buf.at[s], in_sem.at[s])
        for s in range(16)
    ]
    out_copies = [
        pltpu.make_async_copy(
            out_buf.at[s],
            saved_ref.at[source(s) // 2, :, pl.ds((source(s) % 2) * 1024, 1024)],
            out_sem.at[s],
        )
        for s in range(16)
    ]
    for copy in a_copies[:4] + in_copies[:8] + a_copies[4:] + in_copies[8:]:
        copy.start()
    left = lax.dot_general(
        bt_ref[...].astype(jnp.bfloat16),
        rank_order(y, x, core, x_hi, z),
        (((0,), (1,)), ((), ())),
        preferred_element_type=jnp.float32,
    ).astype(jnp.bfloat16)
    for s in range(16):
        k_core, k_y, k_x = s // 8, (s // 2) % 4, s % 2
        if s % 8 == 0:
            for copy in a_copies[4 * k_core : 4 * k_core + 4]:
                copy.wait()
        a_block = jnp.concatenate(
            [
                a_buf[4 * k_core + k_z, k_x_hi, k_y, k_x ^ k_x_hi]
                for k_z in range(4)
                for k_x_hi in range(2)
            ],
            axis=0,
        )
        increment = lax.dot_general(
            left, a_block, (((1,), (0,)), ((), ())), preferred_element_type=jnp.float32
        )
        in_copies[s].wait()
        merged = in_buf[s].astype(jnp.float32) + adapter_factor() * increment
        out_buf[s] = merged.astype(jnp.bfloat16)
        out_copies[s].start()
    for copy in out_copies:
        copy.wait()


def merge(bt_rows, a_parts, arrived):
    return pl.pallas_call(
        merge_kernel,
        in_specs=[pl.BlockSpec(memory_space=pltpu.VMEM)] + [pl.BlockSpec(memory_space=pl.ANY)] * 9,
        out_specs=pl.BlockSpec(memory_space=pl.ANY),
        out_shape=jax.ShapeDtypeStruct((8, 128, 2048), jnp.bfloat16),
        scratch_shapes=[
            pltpu.VMEM((8, 2, 4, 2, 8, 1024), jnp.bfloat16),
            pltpu.VMEM((16, 128, 1024), jnp.bfloat16),
            pltpu.VMEM((16, 128, 1024), jnp.bfloat16),
            pltpu.SemaphoreType.DMA((8,)),
            pltpu.SemaphoreType.DMA((16,)),
            pltpu.SemaphoreType.DMA((16,)),
        ],
        compiler_params=pltpu.CompilerParams(vmem_limit_bytes=56 << 20),
        cost_estimate=pl.CostEstimate(
            flops=2 * 128 * 64 * 16384, bytes_accessed=10 << 20, transcendentals=0
        ),
    )(bt_rows, *a_parts, arrived)


def pick(array, index, axis):
    return lax.dynamic_index_in_dim(array, index, axis, keepdims=False)


def over_core(array):
    return lax.ppermute(array, "col", [(i, i ^ 1) for i in range(16)])


def over_x(array):
    return lax.ppermute(array, "col", [(i, i ^ 2) for i in range(16)])


def over_y(array, k):
    return lax.ppermute(array, "col", [(i, (i + 4 * k) % 16) for i in range(16)])


def over_x_y(array, k_x, k_y):
    return lax.ppermute(array, "col", [(i, ((i + 4 * k_y) % 16) ^ (2 * k_x)) for i in range(16)])


def over_x_hi(array):
    return lax.ppermute(array, "row", [(i, i ^ 4) for i in range(8)])


def over_x_hi_x(array):
    return lax.ppermute(array, ("row", "col"), [(i, i ^ (4 * 16 + 2)) for i in range(128)])


def over_z(array, k):
    return lax.ppermute(array, "row", [(i, i // 4 * 4 + (i + k) % 4) for i in range(8)])


def per_device(
    frozen_projection_weight,
    a_master,
    a_first,
    a_second,
    bt_master,
    bt_first,
    bt_second,
    grad_a_parts,
    grad_bt_parts,
):
    row, col = lax.axis_index("row"), lax.axis_index("col")
    x_hi, z = row // 4, row % 4
    y, x, core = col // 4, (col // 2) % 2, col % 2

    part = grad_a_parts.reshape(2, 4, 8, 1024)
    part = pick(part, z, 1) + sum(over_z(pick(part, (z + k) % 4, 1), k) for k in (1, 2, 3))
    grad_a = pick(part, x_hi, 0) + over_x_hi(pick(part, 1 - x_hi, 0))
    part = grad_bt_parts.reshape(4, 2, 2, 4, 2048)
    part = pick(part, core, 2) + over_core(pick(part, 1 - core, 2))
    part = pick(part, x, 1) + over_x(pick(part, 1 - x, 1))
    grad_bt = pick(part, y, 0) + sum(over_y(pick(part, (y + k) % 4, 0), k) for k in (1, 2, 3))

    a_new, a_first_new, a_second_new = adam_step(a_master, a_first, a_second, grad_a)
    bt_new, bt_first_new, bt_second_new = adam_step(bt_master, bt_first, bt_second, grad_bt)

    part = bt_new.reshape(4, 4, 2, 2, 128).transpose(1, 2, 3, 0, 4)
    part = jnp.concatenate([pick(part, core, 2), over_core(pick(part, 1 - core, 2))], axis=2)
    bt_for = part.astype(jnp.bfloat16)
    a_half = a_new.astype(jnp.bfloat16)
    sent = pick(bt_for, 1 - x, 1).transpose(1, 0, 2).reshape(8, 512)
    came = over_x(jnp.concatenate([a_half, sent], axis=1))
    a_near = jnp.stack([a_half, came[:, :1024]])
    bt_near = jnp.stack([pick(bt_for, x, 1), came[:, 1024:].reshape(8, 4, 128).transpose(1, 0, 2)], axis=1)
    along_y = [
        over_y(jnp.concatenate([a_near, pick(bt_near, (y + k) % 4, 0)], axis=2), k) for k in (1, 2, 3)
    ]
    weight = frozen_projection_weight.reshape(16, 128, 1024)
    weight, *along_y = lax.optimization_barrier((weight, *along_y))
    arrived = lax.all_to_all(weight, "col", 0, 0, tiled=True)
    part = jnp.stack([a_near] + [came[:, :, :1024] for came in along_y])
    bt_rows = jnp.stack([pick(bt_near, y, 0)] + [came[:, :, 1024:] for came in along_y])
    part = jnp.stack([part, over_x_hi_x(part)])
    a_parts = [part] + [over_z(part, k) for k in (1, 2, 3)]
    a_parts = a_parts + [over_core(part) for part in a_parts]
    saved = merge(bt_rows.reshape(R, 128).astype(jnp.float32), a_parts, arrived)
    return (saved, a_new, a_first_new, a_second_new, bt_new, bt_first_new, bt_second_new)


def solution(mesh):
    return jax.shard_map(
        per_device,
        mesh=mesh,
        in_specs=(
            P("row", "col"),
            P("row", "col"),
            P("row", "col"),
            P("row", "col"),
            P("col", "row"),
            P("col", "row"),
            P("col", "row"),
            P("row", None, "col"),
            P("col", None, "row"),
        ),
        out_specs=(
            P(None, ("row", "col"), None),
            P("row", "col"),
            P("row", "col"),
            P("row", "col"),
            P("col", "row"),
            P("col", "row"),
            P("col", "row"),
        ),
        check_vma=False,
    )
```

```python
import math

import jax
import jax.numpy as jnp
from jax import lax
from jax.experimental import pallas as pl
from jax.experimental.pallas import tpu as pltpu
from jax.sharding import PartitionSpec as P

D = 16384
R = 64
TP = 8
STEP = 10


beta_first = 0.9
beta_second = 0.95
adam_eps = 1e-08
learn_rate = 0.08


def adapter_factor():
    return 0.25 / math.sqrt(R * D)


def adam_step(master, first, second, grad):
    first_new = beta_first * first + (1.0 - beta_first) * grad
    second_new = beta_second * second + (1.0 - beta_second) * grad * grad
    corr_first = 1.0 - beta_first**STEP
    corr_second = 1.0 - beta_second**STEP
    update = first_new / corr_first / (jnp.sqrt(second_new / corr_second) + adam_eps)
    return (master - learn_rate * update, first_new, second_new)


def mod4(value):
    return lax.rem(value + 4, 4)


def rank_order(y, x, core, x_hi, z):
    p = lax.broadcasted_iota(jnp.int32, (R, R), 0)
    s = lax.broadcasted_iota(jnp.int32, (R, R), 1)
    from_z = (z - p // 16 + 4) % 4
    from_x_hi = x_hi ^ ((p // 8) % 2)
    rank_a = 8 * (from_x_hi * 4 + from_z) + p % 8
    from_y = (y - s // 16 + 4) % 4
    from_x = x ^ ((s // 8) % 2)
    from_core = core ^ ((s // 4) % 2)
    rank_b = 4 * (from_y * 4 + from_x * 2 + from_core) + s % 4
    return (rank_a == rank_b).astype(jnp.bfloat16)


def merge_kernel(bt_ref, *refs):
    a_refs, arrived_ref, saved_ref = refs[:8], refs[8], refs[9]
    a_buf, in_buf, out_buf, a_sem, in_sem, out_sem = refs[10:]
    row, col = lax.axis_index("row"), lax.axis_index("col")
    x_hi, z = row // 4, row % 4
    y, x, core = col // 4, (col // 2) % 2, col % 2

    def source(step):
        k_core, k_y, k_x = step // 8, (step // 2) % 4, step % 2
        return mod4(y - k_y) * 4 + (x ^ k_x) * 2 + (core ^ k_core)

    a_copies = [pltpu.make_async_copy(a_refs[i], a_buf.at[i], a_sem.at[i]) for i in range(8)]
    in_copies = [
        pltpu.make_async_copy(arrived_ref.at[source(s)], in_buf.at[s], in_sem.at[s])
        for s in range(16)
    ]
    out_copies = [
        pltpu.make_async_copy(
            out_buf.at[s],
            saved_ref.at[source(s) // 2, :, pl.ds((source(s) % 2) * 1024, 1024)],
            out_sem.at[s],
        )
        for s in range(16)
    ]
    for copy in a_copies[:4] + in_copies[:8] + a_copies[4:] + in_copies[8:]:
        copy.start()
    left = lax.dot_general(
        bt_ref[...].astype(jnp.bfloat16),
        rank_order(y, x, core, x_hi, z),
        (((0,), (1,)), ((), ())),
        preferred_element_type=jnp.float32,
    ).astype(jnp.bfloat16)
    for copy in a_copies:
        copy.wait()
    for first in range(0, 16, 4):
        group = range(first, first + 4)
        for s in group:
            in_copies[s].wait()
        for s in group:
            k_core, k_y, k_x = s // 8, (s // 2) % 4, s % 2
            a_block = jnp.concatenate(
                [
                    a_buf[4 * k_core + k_z, k_x_hi, k_y, k_x ^ k_x_hi]
                    for k_z in range(4)
                    for k_x_hi in range(2)
                ],
                axis=0,
            )
            increment = lax.dot_general(
                left, a_block, (((1,), (0,)), ((), ())), preferred_element_type=jnp.float32
            )
            merged = in_buf[s].astype(jnp.float32) + adapter_factor() * increment
            out_buf[s] = merged.astype(jnp.bfloat16)
        for s in group:
            out_copies[s].start()
    for copy in out_copies:
        copy.wait()


def merge(bt_rows, a_parts, arrived):
    return pl.pallas_call(
        merge_kernel,
        in_specs=[pl.BlockSpec(memory_space=pltpu.VMEM)] + [pl.BlockSpec(memory_space=pl.ANY)] * 9,
        out_specs=pl.BlockSpec(memory_space=pl.ANY),
        out_shape=jax.ShapeDtypeStruct((8, 128, 2048), jnp.bfloat16),
        scratch_shapes=[
            pltpu.VMEM((8, 2, 4, 2, 8, 1024), jnp.bfloat16),
            pltpu.VMEM((16, 128, 1024), jnp.bfloat16),
            pltpu.VMEM((16, 128, 1024), jnp.bfloat16),
            pltpu.SemaphoreType.DMA((8,)),
            pltpu.SemaphoreType.DMA((16,)),
            pltpu.SemaphoreType.DMA((16,)),
        ],
        compiler_params=pltpu.CompilerParams(vmem_limit_bytes=32 << 20),
        cost_estimate=pl.CostEstimate(
            flops=2 * 128 * 64 * 16384, bytes_accessed=10 << 20, transcendentals=0
        ),
    )(bt_rows, *a_parts, arrived)


def pick(array, index, axis):
    return lax.dynamic_index_in_dim(array, index, axis, keepdims=False)


def over_core(array):
    return lax.ppermute(array, "col", [(i, i ^ 1) for i in range(16)])


def over_x(array):
    return lax.ppermute(array, "col", [(i, i ^ 2) for i in range(16)])


def over_y(array, k):
    return lax.ppermute(array, "col", [(i, (i + 4 * k) % 16) for i in range(16)])


def over_x_y(array, k_x, k_y):
    return lax.ppermute(array, "col", [(i, ((i + 4 * k_y) % 16) ^ (2 * k_x)) for i in range(16)])


def over_col(array, mask):
    return lax.ppermute(array, "col", [(i, i ^ mask) for i in range(16)])


def over_row(array, mask):
    return lax.ppermute(array, "row", [(i, i ^ mask) for i in range(8)])


def two_of(array, first, second, axis):
    return jnp.stack([pick(array, first, axis), pick(array, second, axis)], axis=axis)


def over_x_hi(array):
    return lax.ppermute(array, "row", [(i, i ^ 4) for i in range(8)])


def over_x_hi_x(array):
    return lax.ppermute(array, ("row", "col"), [(i, i ^ (4 * 16 + 2)) for i in range(128)])


def over_z(array, k):
    return lax.ppermute(array, "row", [(i, i // 4 * 4 + (i + k) % 4) for i in range(8)])


def per_device(
    frozen_projection_weight,
    a_master,
    a_first,
    a_second,
    bt_master,
    bt_first,
    bt_second,
    grad_a_parts,
    grad_bt_parts,
):
    row, col = lax.axis_index("row"), lax.axis_index("col")
    x_hi, z = row // 4, row % 4
    y, x, core = col // 4, (col // 2) % 2, col % 2

    part = grad_a_parts.reshape(2, 4, 8, 1024)
    part = pick(part, z, 1) + sum(over_z(pick(part, (z + k) % 4, 1), k) for k in (1, 2, 3))
    grad_a = pick(part, x_hi, 0) + over_x_hi(pick(part, 1 - x_hi, 0))
    part = grad_bt_parts.reshape(4, 2, 2, 4, 2048)
    part = pick(part, core, 2) + over_core(pick(part, 1 - core, 2))
    part = pick(part, x, 1) + over_x(pick(part, 1 - x, 1))
    grad_bt = pick(part, y, 0) + sum(over_y(pick(part, (y + k) % 4, 0), k) for k in (1, 2, 3))

    a_new, a_first_new, a_second_new = adam_step(a_master, a_first, a_second, grad_a)
    bt_new, bt_first_new, bt_second_new = adam_step(bt_master, bt_first, bt_second, grad_bt)

    part = bt_new.reshape(4, 4, 2, 2, 128).transpose(1, 2, 3, 0, 4)
    part = jnp.concatenate([pick(part, core, 2), over_core(pick(part, 1 - core, 2))], axis=2)
    bt_for = part.astype(jnp.bfloat16)
    a_half = a_new.astype(jnp.bfloat16)
    sent = pick(bt_for, 1 - x, 1).transpose(1, 0, 2).reshape(8, 512)
    came = over_x(jnp.concatenate([a_half, sent], axis=1))
    a_near = jnp.stack([a_half, came[:, :1024]])
    bt_near = jnp.stack([pick(bt_for, x, 1), came[:, 1024:].reshape(8, 4, 128).transpose(1, 0, 2)], axis=1)
    along_y = [
        over_y(jnp.concatenate([a_near, pick(bt_near, (y + k) % 4, 0)], axis=2), k) for k in (1, 2, 3)
    ]
    weight = frozen_projection_weight.reshape(16, 128, 1024)
    weight, *along_y = lax.optimization_barrier((weight, *along_y))
    arrived = lax.all_to_all(weight, "col", 0, 0, tiled=True)
    part = jnp.stack([a_near] + [came[:, :, :1024] for came in along_y])
    bt_rows = jnp.stack([pick(bt_near, y, 0)] + [came[:, :, 1024:] for came in along_y])
    part = jnp.stack([part, over_x_hi_x(part)])
    a_parts = [part] + [over_z(part, k) for k in (1, 2, 3)]
    a_parts = a_parts + [over_core(part) for part in a_parts]
    saved = merge(bt_rows.reshape(R, 128).astype(jnp.float32), a_parts, arrived)
    return (saved, a_new, a_first_new, a_second_new, bt_new, bt_first_new, bt_second_new)


def solution(mesh):
    return jax.shard_map(
        per_device,
        mesh=mesh,
        in_specs=(
            P("row", "col"),
            P("row", "col"),
            P("row", "col"),
            P("row", "col"),
            P("col", "row"),
            P("col", "row"),
            P("col", "row"),
            P("row", None, "col"),
            P("col", None, "row"),
        ),
        out_specs=(
            P(None, ("row", "col"), None),
            P("row", "col"),
            P("row", "col"),
            P("row", "col"),
            P("col", "row"),
            P("col", "row"),
            P("col", "row"),
        ),
        check_vma=False,
    )
```

```python
import math

import jax
import jax.numpy as jnp
from jax import lax
from jax.experimental import pallas as pl
from jax.experimental.pallas import tpu as pltpu
from jax.sharding import PartitionSpec as P

D = 16384
R = 64
TP = 8
STEP = 10


beta_first = 0.9
beta_second = 0.95
adam_eps = 1e-08
learn_rate = 0.08


def adapter_factor():
    return 0.25 / math.sqrt(R * D)


def adam_step(master, first, second, grad):
    first_new = beta_first * first + (1.0 - beta_first) * grad
    second_new = beta_second * second + (1.0 - beta_second) * grad * grad
    corr_first = 1.0 - beta_first**STEP
    corr_second = 1.0 - beta_second**STEP
    update = first_new / corr_first / (jnp.sqrt(second_new / corr_second) + adam_eps)
    return (master - learn_rate * update, first_new, second_new)


def mod4(value):
    return lax.rem(value + 4, 4)


def rank_order(y, x, core, x_hi, z):
    p = lax.broadcasted_iota(jnp.int32, (R, R), 0)
    s = lax.broadcasted_iota(jnp.int32, (R, R), 1)
    from_z = (z - p // 16 + 4) % 4
    from_x_hi = x_hi ^ ((p // 8) % 2)
    rank_a = 8 * (from_x_hi * 4 + from_z) + p % 8
    from_y = (y - s // 16 + 4) % 4
    from_x = x ^ ((s // 8) % 2)
    from_core = core ^ ((s // 4) % 2)
    rank_b = 4 * (from_y * 4 + from_x * 2 + from_core) + s % 4
    return (rank_a == rank_b).astype(jnp.bfloat16)


def merge_kernel(bt_ref, *refs):
    a_refs, arrived_ref, saved_ref = refs[:8], refs[8], refs[9]
    a_buf, in_buf, out_buf, a_sem, in_sem, out_sem = refs[10:]
    row, col = lax.axis_index("row"), lax.axis_index("col")
    x_hi, z = row // 4, row % 4
    y, x, core = col // 4, (col // 2) % 2, col % 2

    def source(step):
        k_core, k_y, k_x = step // 8, (step // 2) % 4, step % 2
        return mod4(y - k_y) * 4 + (x ^ k_x) * 2 + (core ^ k_core)

    a_copies = [pltpu.make_async_copy(a_refs[i], a_buf.at[i], a_sem.at[i]) for i in range(8)]
    in_copies = [
        pltpu.make_async_copy(arrived_ref.at[source(s)], in_buf.at[s], in_sem.at[s])
        for s in range(16)
    ]
    out_copies = [
        pltpu.make_async_copy(
            out_buf.at[s],
            saved_ref.at[source(s) // 2, :, pl.ds((source(s) % 2) * 1024, 1024)],
            out_sem.at[s],
        )
        for s in range(16)
    ]
    for copy in a_copies[:4] + in_copies[:8] + a_copies[4:] + in_copies[8:]:
        copy.start()
    left = lax.dot_general(
        bt_ref[...].astype(jnp.bfloat16),
        rank_order(y, x, core, x_hi, z),
        (((0,), (1,)), ((), ())),
        preferred_element_type=jnp.float32,
    ).astype(jnp.bfloat16)
    for copy in a_copies:
        copy.wait()
    for first in range(0, 16, 4):
        group = range(first, first + 4)
        for s in group:
            in_copies[s].wait()
        for s in group:
            k_core, k_y, k_x = s // 8, (s // 2) % 4, s % 2
            a_block = jnp.concatenate(
                [
                    a_buf[4 * k_core + k_z, k_x_hi, k_y, k_x ^ k_x_hi]
                    for k_z in range(4)
                    for k_x_hi in range(2)
                ],
                axis=0,
            )
            increment = lax.dot_general(
                left, a_block, (((1,), (0,)), ((), ())), preferred_element_type=jnp.float32
            )
            merged = in_buf[s].astype(jnp.float32) + adapter_factor() * increment
            out_buf[s] = merged.astype(jnp.bfloat16)
        for s in group:
            out_copies[s].start()
    for copy in out_copies:
        copy.wait()


def merge(bt_rows, a_parts, arrived):
    return pl.pallas_call(
        merge_kernel,
        in_specs=[pl.BlockSpec(memory_space=pltpu.VMEM)] + [pl.BlockSpec(memory_space=pl.ANY)] * 9,
        out_specs=pl.BlockSpec(memory_space=pl.ANY),
        out_shape=jax.ShapeDtypeStruct((8, 128, 2048), jnp.bfloat16),
        scratch_shapes=[
            pltpu.VMEM((8, 2, 4, 2, 8, 1024), jnp.bfloat16),
            pltpu.VMEM((16, 128, 1024), jnp.bfloat16),
            pltpu.VMEM((16, 128, 1024), jnp.bfloat16),
            pltpu.SemaphoreType.DMA((8,)),
            pltpu.SemaphoreType.DMA((16,)),
            pltpu.SemaphoreType.DMA((16,)),
        ],
        compiler_params=pltpu.CompilerParams(vmem_limit_bytes=32 << 20),
        cost_estimate=pl.CostEstimate(
            flops=2 * 128 * 64 * 16384, bytes_accessed=10 << 20, transcendentals=0
        ),
    )(bt_rows, *a_parts, arrived)


def pick(array, index, axis):
    return lax.dynamic_index_in_dim(array, index, axis, keepdims=False)


def over_core(array):
    return lax.ppermute(array, "col", [(i, i ^ 1) for i in range(16)])


def over_x(array):
    return lax.ppermute(array, "col", [(i, i ^ 2) for i in range(16)])


def over_y(array, k):
    return lax.ppermute(array, "col", [(i, (i + 4 * k) % 16) for i in range(16)])


def over_x_y(array, k_x, k_y):
    return lax.ppermute(array, "col", [(i, ((i + 4 * k_y) % 16) ^ (2 * k_x)) for i in range(16)])


def over_col(array, mask):
    return lax.ppermute(array, "col", [(i, i ^ mask) for i in range(16)])


def over_row(array, mask):
    return lax.ppermute(array, "row", [(i, i ^ mask) for i in range(8)])


def two_of(array, first, second, axis):
    return jnp.stack([pick(array, first, axis), pick(array, second, axis)], axis=axis)


def over_x_hi(array):
    return lax.ppermute(array, "row", [(i, i ^ 4) for i in range(8)])


def over_x_hi_x(array):
    return lax.ppermute(array, ("row", "col"), [(i, i ^ (4 * 16 + 2)) for i in range(128)])


def over_z(array, k):
    return lax.ppermute(array, "row", [(i, i // 4 * 4 + (i + k) % 4) for i in range(8)])


def per_device(
    frozen_projection_weight,
    a_master,
    a_first,
    a_second,
    bt_master,
    bt_first,
    bt_second,
    grad_a_parts,
    grad_bt_parts,
):
    row, col = lax.axis_index("row"), lax.axis_index("col")
    x_hi, z = row // 4, row % 4
    y, x, core = col // 4, (col // 2) % 2, col % 2

    bt_part = grad_bt_parts.reshape(4, 2, 2, 4, 2048)
    kept, sent = lax.optimization_barrier((pick(bt_part, core, 2), pick(bt_part, 1 - core, 2)))
    bt_part = kept + over_core(sent)
    part = grad_a_parts.reshape(2, 4, 8, 1024)
    kept, *sent = lax.optimization_barrier([pick(part, (z + k) % 4, 1) for k in range(4)])
    bt_part, *sent = lax.optimization_barrier((bt_part, *sent))
    part = kept + sum(over_z(array, k) for array, k in zip(sent, (1, 2, 3)))
    grad_a = pick(part, x_hi, 0) + over_x_hi(pick(part, 1 - x_hi, 0))
    bt_part = pick(bt_part, x, 1) + over_x(pick(bt_part, 1 - x, 1))
    bt_part = two_of(bt_part, y, y ^ 3, 0) + over_col(two_of(bt_part, y ^ 1, y ^ 2, 0), 4)
    grad_bt = bt_part[0] + over_col(bt_part[1], 12)

    a_new = adam_step(a_master, a_first, a_second, grad_a)[0]
    bt_new = adam_step(bt_master, bt_first, bt_second, grad_bt)[0]

    part = bt_new.reshape(4, 4, 2, 2, 128).transpose(1, 2, 3, 0, 4)
    part = jnp.concatenate([pick(part, core, 2), over_core(pick(part, 1 - core, 2))], axis=2)
    bt_for = part.astype(jnp.bfloat16)
    a_half = a_new.astype(jnp.bfloat16)
    sent = pick(bt_for, 1 - x, 1).transpose(1, 0, 2).reshape(8, 512)
    came = over_x(jnp.concatenate([a_half, sent], axis=1))
    a_near = jnp.stack([a_half, came[:, :1024]])
    bt_near = jnp.stack([pick(bt_for, x, 1), came[:, 1024:].reshape(8, 4, 128).transpose(1, 0, 2)], axis=1)
    along_y = [
        over_y(jnp.concatenate([a_near, pick(bt_near, (y + k) % 4, 0)], axis=2), k) for k in (1, 2, 3)
    ]
    weight = frozen_projection_weight.reshape(16, 128, 1024)
    weight, grad_a, grad_bt, *along_y = lax.optimization_barrier((weight, grad_a, grad_bt, *along_y))
    arrived = lax.all_to_all(weight, "col", 0, 0, tiled=True)
    part = jnp.stack([a_near] + [came[:, :, :1024] for came in along_y])
    bt_rows = jnp.stack([pick(bt_near, y, 0)] + [came[:, :, 1024:] for came in along_y])
    part = jnp.stack([part, over_x_hi_x(part)])
    a_parts = [part] + [over_z(part, k) for k in (1, 2, 3)]
    a_parts = a_parts + [over_core(part) for part in a_parts]
    saved = merge(bt_rows.reshape(R, 128).astype(jnp.float32), a_parts, arrived)
    a_new, a_first_new, a_second_new = adam_step(a_master, a_first, a_second, grad_a)
    bt_new, bt_first_new, bt_second_new = adam_step(bt_master, bt_first, bt_second, grad_bt)
    return (saved, a_new, a_first_new, a_second_new, bt_new, bt_first_new, bt_second_new)


def solution(mesh):
    return jax.shard_map(
        per_device,
        mesh=mesh,
        in_specs=(
            P("row", "col"),
            P("row", "col"),
            P("row", "col"),
            P("row", "col"),
            P("col", "row"),
            P("col", "row"),
            P("col", "row"),
            P("row", None, "col"),
            P("col", None, "row"),
        ),
        out_specs=(
            P(None, ("row", "col"), None),
            P("row", "col"),
            P("row", "col"),
            P("row", "col"),
            P("col", "row"),
            P("col", "row"),
            P("col", "row"),
        ),
        check_vma=False,
    )
```

```python
import math

import jax
import jax.numpy as jnp
from jax import lax
from jax.experimental import pallas as pl
from jax.experimental.pallas import tpu as pltpu
from jax.sharding import PartitionSpec as P

D = 16384
R = 64
TP = 8
STEP = 10


beta_first = 0.9
beta_second = 0.95
adam_eps = 1e-08
learn_rate = 0.08


def adapter_factor():
    return 0.25 / math.sqrt(R * D)


def adam_step(master, first, second, grad):
    first_new = beta_first * first + (1.0 - beta_first) * grad
    second_new = beta_second * second + (1.0 - beta_second) * grad * grad
    corr_first = 1.0 - beta_first**STEP
    corr_second = 1.0 - beta_second**STEP
    update = first_new / corr_first / (jnp.sqrt(second_new / corr_second) + adam_eps)
    return (master - learn_rate * update, first_new, second_new)


def mod4(value):
    return lax.rem(value + 4, 4)


def rank_order(y, x, core, x_hi, z):
    p = lax.broadcasted_iota(jnp.int32, (R, R), 0)
    s = lax.broadcasted_iota(jnp.int32, (R, R), 1)
    from_z = (z - p // 16 + 4) % 4
    from_x_hi = x_hi ^ ((p // 8) % 2)
    rank_a = 8 * (from_x_hi * 4 + from_z) + p % 8
    from_y = (y - s // 16 + 4) % 4
    from_x = x ^ ((s // 8) % 2)
    from_core = core ^ ((s // 4) % 2)
    rank_b = 4 * (from_y * 4 + from_x * 2 + from_core) + s % 4
    return (rank_a == rank_b).astype(jnp.bfloat16)


def merge_kernel(bt_ref, *refs):
    a_refs, arrived_ref, saved_ref = refs[:8], refs[8], refs[9]
    a_buf, in_buf, out_buf, a_sem, in_sem, out_sem = refs[10:]
    row, col = lax.axis_index("row"), lax.axis_index("col")
    x_hi, z = row // 4, row % 4
    y, x, core = col // 4, (col // 2) % 2, col % 2

    def source(step):
        k_core, k_y, k_x = step // 8, (step // 2) % 4, step % 2
        return mod4(y - k_y) * 4 + (x ^ k_x) * 2 + (core ^ k_core)

    a_copies = [pltpu.make_async_copy(a_refs[i], a_buf.at[i], a_sem.at[i]) for i in range(8)]
    in_copies = [
        pltpu.make_async_copy(arrived_ref.at[source(s)], in_buf.at[s], in_sem.at[s])
        for s in range(16)
    ]
    out_copies = [
        pltpu.make_async_copy(
            out_buf.at[s],
            saved_ref.at[source(s) // 2, :, pl.ds((source(s) % 2) * 1024, 1024)],
            out_sem.at[s],
        )
        for s in range(16)
    ]
    for copy in a_copies[:4] + in_copies[:8] + a_copies[4:] + in_copies[8:]:
        copy.start()
    left = lax.dot_general(
        bt_ref[...].astype(jnp.bfloat16),
        rank_order(y, x, core, x_hi, z),
        (((0,), (1,)), ((), ())),
        preferred_element_type=jnp.float32,
    ).astype(jnp.bfloat16)
    for copy in a_copies:
        copy.wait()
    for first in range(0, 16, 4):
        group = range(first, first + 4)
        for s in group:
            in_copies[s].wait()
        for s in group:
            k_core, k_y, k_x = s // 8, (s // 2) % 4, s % 2
            a_block = jnp.concatenate(
                [
                    a_buf[4 * k_core + k_z, k_x_hi, k_y, k_x ^ k_x_hi]
                    for k_z in range(4)
                    for k_x_hi in range(2)
                ],
                axis=0,
            )
            increment = lax.dot_general(
                left, a_block, (((1,), (0,)), ((), ())), preferred_element_type=jnp.float32
            )
            merged = in_buf[s].astype(jnp.float32) + adapter_factor() * increment
            out_buf[s] = merged.astype(jnp.bfloat16)
        for s in group:
            out_copies[s].start()
    for copy in out_copies:
        copy.wait()


def merge(bt_rows, a_parts, arrived):
    return pl.pallas_call(
        merge_kernel,
        in_specs=[pl.BlockSpec(memory_space=pltpu.VMEM)] + [pl.BlockSpec(memory_space=pl.ANY)] * 9,
        out_specs=pl.BlockSpec(memory_space=pl.ANY),
        out_shape=jax.ShapeDtypeStruct((8, 128, 2048), jnp.bfloat16),
        scratch_shapes=[
            pltpu.VMEM((8, 2, 4, 2, 8, 1024), jnp.bfloat16),
            pltpu.VMEM((16, 128, 1024), jnp.bfloat16),
            pltpu.VMEM((16, 128, 1024), jnp.bfloat16),
            pltpu.SemaphoreType.DMA((8,)),
            pltpu.SemaphoreType.DMA((16,)),
            pltpu.SemaphoreType.DMA((16,)),
        ],
        compiler_params=pltpu.CompilerParams(vmem_limit_bytes=32 << 20),
        cost_estimate=pl.CostEstimate(
            flops=2 * 128 * 64 * 16384, bytes_accessed=10 << 20, transcendentals=0
        ),
    )(bt_rows, *a_parts, arrived)


def hold_kernel(array_ref, held_ref):
    held_ref[...] = array_ref[...]


def hold(array):
    return pl.pallas_call(
        hold_kernel,
        out_shape=jax.ShapeDtypeStruct(array.shape, array.dtype),
        cost_estimate=pl.CostEstimate(flops=100000000000, bytes_accessed=1 << 18, transcendentals=0),
    )(array)


def pick(array, index, axis):
    return lax.dynamic_index_in_dim(array, index, axis, keepdims=False)


def over_core(array):
    return lax.ppermute(array, "col", [(i, i ^ 1) for i in range(16)])


def over_x(array):
    return lax.ppermute(array, "col", [(i, i ^ 2) for i in range(16)])


def over_y(array, k):
    return lax.ppermute(array, "col", [(i, (i + 4 * k) % 16) for i in range(16)])


def over_x_y(array, k_x, k_y):
    return lax.ppermute(array, "col", [(i, ((i + 4 * k_y) % 16) ^ (2 * k_x)) for i in range(16)])


def over_col(array, mask):
    return lax.ppermute(array, "col", [(i, i ^ mask) for i in range(16)])


def over_row(array, mask):
    return lax.ppermute(array, "row", [(i, i ^ mask) for i in range(8)])


def two_of(array, first, second, axis):
    return jnp.stack([pick(array, first, axis), pick(array, second, axis)], axis=axis)


def over_x_hi(array):
    return lax.ppermute(array, "row", [(i, i ^ 4) for i in range(8)])


def over_x_hi_x(array):
    return lax.ppermute(array, ("row", "col"), [(i, i ^ (4 * 16 + 2)) for i in range(128)])


def over_z(array, k):
    return lax.ppermute(array, "row", [(i, i // 4 * 4 + (i + k) % 4) for i in range(8)])


def per_device(
    frozen_projection_weight,
    a_master,
    a_first,
    a_second,
    bt_master,
    bt_first,
    bt_second,
    grad_a_parts,
    grad_bt_parts,
):
    row, col = lax.axis_index("row"), lax.axis_index("col")
    x_hi, z = row // 4, row % 4
    y, x, core = col // 4, (col // 2) % 2, col % 2

    bt_part = grad_bt_parts.reshape(4, 2, 2, 4, 2048)
    kept, sent = lax.optimization_barrier((pick(bt_part, core, 2), pick(bt_part, 1 - core, 2)))
    bt_part = kept + over_core(sent)
    part = grad_a_parts.reshape(2, 4, 8, 1024)
    kept, *sent = lax.optimization_barrier([pick(part, (z + k) % 4, 1) for k in range(4)])
    bt_part, *sent = lax.optimization_barrier((bt_part, *sent))
    part = kept + sum(over_z(array, k) for array, k in zip(sent, (1, 2, 3)))
    grad_a = pick(part, x_hi, 0) + over_x_hi(pick(part, 1 - x_hi, 0))
    bt_part = pick(bt_part, x, 1) + over_x(pick(bt_part, 1 - x, 1))
    bt_part = two_of(bt_part, y, y ^ 3, 0) + over_col(two_of(bt_part, y ^ 1, y ^ 2, 0), 4)
    grad_bt = bt_part[0] + over_col(bt_part[1], 12)

    a_new = adam_step(a_master, a_first, a_second, grad_a)[0]
    bt_new = adam_step(bt_master, bt_first, bt_second, grad_bt)[0]

    part = bt_new.reshape(4, 4, 2, 2, 128).transpose(1, 2, 3, 0, 4)
    part = jnp.concatenate([pick(part, core, 2), over_core(pick(part, 1 - core, 2))], axis=2)
    bt_for = part.astype(jnp.bfloat16)
    a_half = a_new.astype(jnp.bfloat16)
    sent = pick(bt_for, 1 - x, 1).transpose(1, 0, 2).reshape(8, 512)
    came = over_x(jnp.concatenate([a_half, sent], axis=1))
    a_near = jnp.stack([a_half, came[:, :1024]])
    bt_near = jnp.stack([pick(bt_for, x, 1), came[:, 1024:].reshape(8, 4, 128).transpose(1, 0, 2)], axis=1)
    along_y = [
        over_y(jnp.concatenate([a_near, pick(bt_near, (y + k) % 4, 0)], axis=2), k) for k in (1, 2, 3)
    ]
    weight = frozen_projection_weight.reshape(16, 128, 1024)
    weight, grad_a, grad_bt, a_near = lax.optimization_barrier((weight, grad_a, grad_bt, a_near))
    arrived = lax.all_to_all(weight, "col", 0, 0, tiled=True)
    part = jnp.stack([a_near] + [came[:, :, :1024] for came in along_y])
    bt_rows = jnp.stack([pick(bt_near, y, 0)] + [came[:, :, 1024:] for came in along_y])
    part = hold(part)
    part = jnp.stack([part, over_x_hi_x(part)])
    a_parts = [part] + [over_z(part, k) for k in (1, 2, 3)]
    a_parts = a_parts + [over_core(part) for part in a_parts]
    saved = merge(bt_rows.reshape(R, 128).astype(jnp.float32), a_parts, arrived)
    a_new, a_first_new, a_second_new = adam_step(a_master, a_first, a_second, grad_a)
    bt_new, bt_first_new, bt_second_new = adam_step(bt_master, bt_first, bt_second, grad_bt)
    return (saved, a_new, a_first_new, a_second_new, bt_new, bt_first_new, bt_second_new)


def solution(mesh):
    return jax.shard_map(
        per_device,
        mesh=mesh,
        in_specs=(
            P("row", "col"),
            P("row", "col"),
            P("row", "col"),
            P("row", "col"),
            P("col", "row"),
            P("col", "row"),
            P("col", "row"),
            P("row", None, "col"),
            P("col", None, "row"),
        ),
        out_specs=(
            P(None, ("row", "col"), None),
            P("row", "col"),
            P("row", "col"),
            P("row", "col"),
            P("col", "row"),
            P("col", "row"),
            P("col", "row"),
        ),
        check_vma=False,
    )
```

```python
import math

import jax
import jax.numpy as jnp
from jax import lax
from jax.experimental import pallas as pl
from jax.experimental.pallas import tpu as pltpu
from jax.sharding import PartitionSpec as P

D = 16384
R = 64
TP = 8
STEP = 10


beta_first = 0.9
beta_second = 0.95
adam_eps = 1e-08
learn_rate = 0.08


def adapter_factor():
    return 0.25 / math.sqrt(R * D)


def adam_step(master, first, second, grad):
    first_new = beta_first * first + (1.0 - beta_first) * grad
    second_new = beta_second * second + (1.0 - beta_second) * grad * grad
    corr_first = 1.0 - beta_first**STEP
    corr_second = 1.0 - beta_second**STEP
    update = first_new / corr_first / (jnp.sqrt(second_new / corr_second) + adam_eps)
    return (master - learn_rate * update, first_new, second_new)


def mod4(value):
    return lax.rem(value + 4, 4)


def rank_order(y, x, core, x_hi, z):
    p = lax.broadcasted_iota(jnp.int32, (R, R), 0)
    s = lax.broadcasted_iota(jnp.int32, (R, R), 1)
    from_z = (z - p // 16 + 4) % 4
    from_x_hi = x_hi ^ ((p // 8) % 2)
    rank_a = 8 * (from_x_hi * 4 + from_z) + p % 8
    from_y = (y - s // 16 + 4) % 4
    from_x = x ^ ((s // 8) % 2)
    from_core = core ^ ((s // 4) % 2)
    rank_b = 4 * (from_y * 4 + from_x * 2 + from_core) + s % 4
    return (rank_a == rank_b).astype(jnp.bfloat16)


def merge_kernel(bt_ref, *refs):
    a_refs, arrived_ref, saved_ref = refs[:8], refs[8], refs[9]
    a_buf, in_buf, out_buf, a_sem, in_sem, out_sem = refs[10:]
    row, col = lax.axis_index("row"), lax.axis_index("col")
    x_hi, z = row // 4, row % 4
    y, x, core = col // 4, (col // 2) % 2, col % 2

    def source(step):
        k_core, k_y, k_x = step // 8, (step // 2) % 4, step % 2
        return mod4(y - k_y) * 4 + (x ^ k_x) * 2 + (core ^ k_core)

    a_copies = [pltpu.make_async_copy(a_refs[i], a_buf.at[i], a_sem.at[i]) for i in range(8)]
    in_copies = [
        pltpu.make_async_copy(arrived_ref.at[source(s)], in_buf.at[s], in_sem.at[s])
        for s in range(16)
    ]
    out_copies = [
        pltpu.make_async_copy(
            out_buf.at[s],
            saved_ref.at[source(s) // 2, :, pl.ds((source(s) % 2) * 1024, 1024)],
            out_sem.at[s],
        )
        for s in range(16)
    ]
    for copy in a_copies[:4] + in_copies[:8] + a_copies[4:] + in_copies[8:]:
        copy.start()
    left = lax.dot_general(
        bt_ref[...].astype(jnp.bfloat16),
        rank_order(y, x, core, x_hi, z),
        (((0,), (1,)), ((), ())),
        preferred_element_type=jnp.float32,
    ).astype(jnp.bfloat16)
    for copy in a_copies:
        copy.wait()
    for first in range(0, 16, 4):
        group = range(first, first + 4)
        for s in group:
            in_copies[s].wait()
        for s in group:
            k_core, k_y, k_x = s // 8, (s // 2) % 4, s % 2
            a_block = jnp.concatenate(
                [a_buf[4 * k_core + k_z, k_y, k_x] for k_z in range(4)], axis=0
            )
            increment = lax.dot_general(
                left, a_block, (((1,), (0,)), ((), ())), preferred_element_type=jnp.float32
            )
            merged = in_buf[s].astype(jnp.float32) + adapter_factor() * increment
            out_buf[s] = merged.astype(jnp.bfloat16)
        for s in group:
            out_copies[s].start()
    for copy in out_copies:
        copy.wait()


def merge(bt_rows, a_parts, arrived):
    return pl.pallas_call(
        merge_kernel,
        in_specs=[pl.BlockSpec(memory_space=pltpu.VMEM)] + [pl.BlockSpec(memory_space=pl.ANY)] * 9,
        out_specs=pl.BlockSpec(memory_space=pl.ANY),
        out_shape=jax.ShapeDtypeStruct((8, 128, 2048), jnp.bfloat16),
        scratch_shapes=[
            pltpu.VMEM((8, 4, 2, 16, 1024), jnp.bfloat16),
            pltpu.VMEM((16, 128, 1024), jnp.bfloat16),
            pltpu.VMEM((16, 128, 1024), jnp.bfloat16),
            pltpu.SemaphoreType.DMA((8,)),
            pltpu.SemaphoreType.DMA((16,)),
            pltpu.SemaphoreType.DMA((16,)),
        ],
        compiler_params=pltpu.CompilerParams(vmem_limit_bytes=16 << 20),
        cost_estimate=pl.CostEstimate(
            flops=2 * 128 * 64 * 16384, bytes_accessed=10 << 20, transcendentals=0
        ),
    )(bt_rows, *a_parts, arrived)


def hold_kernel(array_ref, held_ref):
    held_ref[...] = array_ref[...]


def hold(array):
    return pl.pallas_call(
        hold_kernel,
        out_shape=jax.ShapeDtypeStruct(array.shape, array.dtype),
        cost_estimate=pl.CostEstimate(flops=100000000000, bytes_accessed=1 << 18, transcendentals=0),
    )(array)


def pick(array, index, axis):
    return lax.dynamic_index_in_dim(array, index, axis, keepdims=False)


def over_core(array):
    return lax.ppermute(array, "col", [(i, i ^ 1) for i in range(16)])


def over_x(array):
    return lax.ppermute(array, "col", [(i, i ^ 2) for i in range(16)])


def over_y(array, k):
    return lax.ppermute(array, "col", [(i, (i + 4 * k) % 16) for i in range(16)])


def over_x_y(array, k_x, k_y):
    return lax.ppermute(array, "col", [(i, ((i + 4 * k_y) % 16) ^ (2 * k_x)) for i in range(16)])


def over_col(array, mask):
    return lax.ppermute(array, "col", [(i, i ^ mask) for i in range(16)])


def over_row(array, mask):
    return lax.ppermute(array, "row", [(i, i ^ mask) for i in range(8)])


def two_of(array, first, second, axis):
    return jnp.stack([pick(array, first, axis), pick(array, second, axis)], axis=axis)


def over_x_hi(array):
    return lax.ppermute(array, "row", [(i, i ^ 4) for i in range(8)])


def over_x_hi_x(array):
    return lax.ppermute(array, ("row", "col"), [(i, i ^ (4 * 16 + 2)) for i in range(128)])


def over_z(array, k):
    return lax.ppermute(array, "row", [(i, i // 4 * 4 + (i + k) % 4) for i in range(8)])


def per_device(
    frozen_projection_weight,
    a_master,
    a_first,
    a_second,
    bt_master,
    bt_first,
    bt_second,
    grad_a_parts,
    grad_bt_parts,
):
    row, col = lax.axis_index("row"), lax.axis_index("col")
    x_hi, z = row // 4, row % 4
    y, x, core = col // 4, (col // 2) % 2, col % 2

    bt_part = grad_bt_parts.reshape(4, 2, 2, 4, 2048)
    kept, sent = lax.optimization_barrier((pick(bt_part, core, 2), pick(bt_part, 1 - core, 2)))
    bt_part = kept + over_core(sent)
    part = grad_a_parts.reshape(2, 4, 8, 1024)
    kept, *sent = lax.optimization_barrier([pick(part, (z + k) % 4, 1) for k in range(4)])
    bt_part, *sent = lax.optimization_barrier((bt_part, *sent))
    part = kept + sum(over_z(array, k) for array, k in zip(sent, (1, 2, 3)))
    grad_a = pick(part, x_hi, 0) + over_x_hi(pick(part, 1 - x_hi, 0))
    bt_part = two_of(bt_part, y, y ^ 1, 0) + over_col(two_of(bt_part, y ^ 3, y ^ 2, 0), 12)
    bt_part = bt_part[0] + over_col(bt_part[1], 4)
    grad_bt = pick(bt_part, x, 0) + over_x(pick(bt_part, 1 - x, 0))

    a_new = adam_step(a_master, a_first, a_second, grad_a)[0]
    bt_new = adam_step(bt_master, bt_first, bt_second, grad_bt)[0]

    part = bt_new.reshape(4, 4, 2, 2, 128).transpose(1, 2, 3, 0, 4)
    part = jnp.concatenate([pick(part, core, 2), over_core(pick(part, 1 - core, 2))], axis=2)
    bt_for = part.astype(jnp.bfloat16)
    a_half = a_new.astype(jnp.bfloat16)
    sent = pick(bt_for, 1 - x, 1).transpose(1, 0, 2).reshape(8, 512)
    came = over_x(jnp.concatenate([a_half, sent], axis=1))
    a_near = jnp.stack([a_half, came[:, :1024]])
    bt_near = jnp.stack([pick(bt_for, x, 1), came[:, 1024:].reshape(8, 4, 128).transpose(1, 0, 2)], axis=1)
    along_y = [
        over_y(jnp.concatenate([a_near, pick(bt_near, (y + k) % 4, 0)], axis=2), k) for k in (1, 2, 3)
    ]
    weight = frozen_projection_weight.reshape(16, 128, 1024)
    weight, grad_a, grad_bt, a_near = lax.optimization_barrier((weight, grad_a, grad_bt, a_near))
    arrived = lax.all_to_all(weight, "col", 0, 0, tiled=True)
    part = jnp.stack([a_near] + [came[:, :, :1024] for came in along_y])
    bt_rows = jnp.stack([pick(bt_near, y, 0)] + [came[:, :, 1024:] for came in along_y])
    part = hold(part.reshape(64, 1024)).reshape(4, 2, 8, 1024)
    part = jnp.stack([part, over_x_hi_x(part)[:, ::-1]], axis=2).reshape(4, 2, 16, 1024)
    a_parts = [part] + [over_z(part, k) for k in (1, 2, 3)]
    a_parts = a_parts + [over_core(part) for part in a_parts]
    saved = merge(bt_rows.reshape(R, 128).astype(jnp.float32), a_parts, arrived)
    a_new, a_first_new, a_second_new = adam_step(a_master, a_first, a_second, grad_a)
    bt_new, bt_first_new, bt_second_new = adam_step(bt_master, bt_first, bt_second, grad_bt)
    return (saved, a_new, a_first_new, a_second_new, bt_new, bt_first_new, bt_second_new)


def solution(mesh):
    return jax.shard_map(
        per_device,
        mesh=mesh,
        in_specs=(
            P("row", "col"),
            P("row", "col"),
            P("row", "col"),
            P("row", "col"),
            P("col", "row"),
            P("col", "row"),
            P("col", "row"),
            P("row", None, "col"),
            P("col", None, "row"),
        ),
        out_specs=(
            P(None, ("row", "col"), None),
            P("row", "col"),
            P("row", "col"),
            P("row", "col"),
            P("col", "row"),
            P("col", "row"),
            P("col", "row"),
        ),
        check_vma=False,
    )
```

```python
import math

import jax
import jax.numpy as jnp
from jax import lax
from jax.experimental import pallas as pl
from jax.experimental.pallas import tpu as pltpu
from jax.sharding import PartitionSpec as P

D = 16384
R = 64
TP = 8
STEP = 10


beta_first = 0.9
beta_second = 0.95
adam_eps = 1e-08
learn_rate = 0.08


def adapter_factor():
    return 0.25 / math.sqrt(R * D)


def adam_step(master, first, second, grad):
    first_new = beta_first * first + (1.0 - beta_first) * grad
    second_new = beta_second * second + (1.0 - beta_second) * grad * grad
    corr_first = 1.0 - beta_first**STEP
    corr_second = 1.0 - beta_second**STEP
    update = first_new / corr_first / (jnp.sqrt(second_new / corr_second) + adam_eps)
    return (master - learn_rate * update, first_new, second_new)


def mod4(value):
    return lax.rem(value + 4, 4)


def rank_order(y, x, core, x_hi, z):
    p = lax.broadcasted_iota(jnp.int32, (R, R), 0)
    s = lax.broadcasted_iota(jnp.int32, (R, R), 1)
    from_z = (z - p // 16 + 4) % 4
    from_x_hi = x_hi ^ ((p // 8) % 2)
    rank_a = 8 * (from_x_hi * 4 + from_z) + p % 8
    from_y = (y - s // 16 + 4) % 4
    from_x = x ^ ((s // 8) % 2)
    from_core = core ^ ((s // 4) % 2)
    rank_b = 4 * (from_y * 4 + from_x * 2 + from_core) + s % 4
    return (rank_a == rank_b).astype(jnp.bfloat16)


def merge_kernel(bt_ref, *refs):
    a_refs, arrived_ref, saved_ref = refs[:8], refs[8], refs[9]
    a_buf, in_buf, out_buf, a_sem, in_sem, out_sem = refs[10:]
    row, col = lax.axis_index("row"), lax.axis_index("col")
    x_hi, z = row // 4, row % 4
    y, x, core = col // 4, (col // 2) % 2, col % 2

    def source(step):
        k_core, k_y, k_x = step // 8, (step // 2) % 4, step % 2
        return mod4(y - k_y) * 4 + (x ^ k_x) * 2 + (core ^ k_core)

    a_copies = [pltpu.make_async_copy(a_refs[i], a_buf.at[i], a_sem.at[i]) for i in range(8)]
    in_copies = [
        pltpu.make_async_copy(arrived_ref.at[source(s)], in_buf.at[s], in_sem.at[s])
        for s in range(16)
    ]
    out_copies = [
        pltpu.make_async_copy(
            out_buf.at[s],
            saved_ref.at[source(s) // 2, :, pl.ds((source(s) % 2) * 1024, 1024)],
            out_sem.at[s],
        )
        for s in range(16)
    ]
    for copy in a_copies[:4] + in_copies[:8] + a_copies[4:] + in_copies[8:]:
        copy.start()
    left = lax.dot_general(
        bt_ref[...].astype(jnp.bfloat16),
        rank_order(y, x, core, x_hi, z),
        (((0,), (1,)), ((), ())),
        preferred_element_type=jnp.float32,
    ).astype(jnp.bfloat16)
    for copy in a_copies:
        copy.wait()
    for first in range(0, 16, 4):
        group = range(first, first + 4)
        for s in group:
            in_copies[s].wait()
        for s in group:
            k_core, k_y, k_x = s // 8, (s // 2) % 4, s % 2
            a_block = jnp.concatenate(
                [a_buf[4 * k_core + k_z, k_y, k_x] for k_z in range(4)], axis=0
            )
            increment = lax.dot_general(
                left, a_block, (((1,), (0,)), ((), ())), preferred_element_type=jnp.float32
            )
            merged = in_buf[s].astype(jnp.float32) + adapter_factor() * increment
            out_buf[s] = merged.astype(jnp.bfloat16)
        for s in group:
            out_copies[s].start()
    for copy in out_copies:
        copy.wait()


def merge(bt_rows, a_parts, arrived):
    return pl.pallas_call(
        merge_kernel,
        in_specs=[pl.BlockSpec(memory_space=pltpu.VMEM)] + [pl.BlockSpec(memory_space=pl.ANY)] * 9,
        out_specs=pl.BlockSpec(memory_space=pl.ANY),
        out_shape=jax.ShapeDtypeStruct((8, 128, 2048), jnp.bfloat16),
        scratch_shapes=[
            pltpu.VMEM((8, 4, 2, 16, 1024), jnp.bfloat16),
            pltpu.VMEM((16, 128, 1024), jnp.bfloat16),
            pltpu.VMEM((16, 128, 1024), jnp.bfloat16),
            pltpu.SemaphoreType.DMA((8,)),
            pltpu.SemaphoreType.DMA((16,)),
            pltpu.SemaphoreType.DMA((16,)),
        ],
        compiler_params=pltpu.CompilerParams(vmem_limit_bytes=16 << 20),
        cost_estimate=pl.CostEstimate(
            flops=2 * 128 * 64 * 16384, bytes_accessed=10 << 20, transcendentals=0
        ),
    )(bt_rows, *a_parts, arrived)


def hold_kernel(array_ref, held_ref):
    held_ref[...] = array_ref[...]


def hold(array):
    return pl.pallas_call(
        hold_kernel,
        out_shape=jax.ShapeDtypeStruct(array.shape, array.dtype),
        cost_estimate=pl.CostEstimate(flops=100000000000, bytes_accessed=1 << 18, transcendentals=0),
    )(array)


def pick(array, index, axis):
    return lax.dynamic_index_in_dim(array, index, axis, keepdims=False)


def over_core(array):
    return lax.ppermute(array, "col", [(i, i ^ 1) for i in range(16)])


def over_x(array):
    return lax.ppermute(array, "col", [(i, i ^ 2) for i in range(16)])


def over_y(array, k):
    return lax.ppermute(array, "col", [(i, (i + 4 * k) % 16) for i in range(16)])


def over_x_y(array, k_x, k_y):
    return lax.ppermute(array, "col", [(i, ((i + 4 * k_y) % 16) ^ (2 * k_x)) for i in range(16)])


def over_col(array, mask):
    return lax.ppermute(array, "col", [(i, i ^ mask) for i in range(16)])


def over_row(array, mask):
    return lax.ppermute(array, "row", [(i, i ^ mask) for i in range(8)])


def two_of(array, first, second, axis):
    return jnp.stack([pick(array, first, axis), pick(array, second, axis)], axis=axis)


def over_x_hi(array):
    return lax.ppermute(array, "row", [(i, i ^ 4) for i in range(8)])


def over_x_hi_x(array):
    return lax.ppermute(array, ("row", "col"), [(i, i ^ (4 * 16 + 2)) for i in range(128)])


def over_z(array, k):
    return lax.ppermute(array, "row", [(i, i // 4 * 4 + (i + k) % 4) for i in range(8)])


def per_device(
    frozen_projection_weight,
    a_master,
    a_first,
    a_second,
    bt_master,
    bt_first,
    bt_second,
    grad_a_parts,
    grad_bt_parts,
):
    row, col = lax.axis_index("row"), lax.axis_index("col")
    x_hi, z = row // 4, row % 4
    y, x, core = col // 4, (col // 2) % 2, col % 2

    bt_part = grad_bt_parts.reshape(4, 2, 2, 4, 2048)
    kept, sent = lax.optimization_barrier((pick(bt_part, core, 2), pick(bt_part, 1 - core, 2)))
    bt_part = kept + over_core(sent)
    part = grad_a_parts.reshape(2, 4, 8, 1024)
    kept, *sent = lax.optimization_barrier([pick(part, (z + k) % 4, 1) for k in range(4)])
    bt_part, *sent = lax.optimization_barrier((bt_part, *sent))
    part = kept + sum(over_z(sent[k - 1], k) for k in (3, 2, 1))
    grad_a = pick(part, x_hi, 0) + over_x_hi(pick(part, 1 - x_hi, 0))
    bt_part = two_of(bt_part, y, y ^ 1, 0) + over_col(two_of(bt_part, y ^ 3, y ^ 2, 0), 12)
    bt_part = bt_part[0] + over_col(bt_part[1], 4)
    grad_bt = pick(bt_part, x, 0) + over_x(pick(bt_part, 1 - x, 0))

    a_new = adam_step(a_master, a_first, a_second, grad_a)[0]
    bt_new = adam_step(bt_master, bt_first, bt_second, grad_bt)[0]

    part = bt_new.reshape(4, 4, 2, 2, 128).transpose(1, 2, 3, 0, 4)
    part = jnp.concatenate([pick(part, core, 2), over_core(pick(part, 1 - core, 2))], axis=2)
    bt_for = part.astype(jnp.bfloat16)
    a_half = a_new.astype(jnp.bfloat16)
    sent = pick(bt_for, 1 - x, 1).transpose(1, 0, 2).reshape(8, 512)
    came = over_x(jnp.concatenate([a_half, sent], axis=1))
    a_near = jnp.stack([a_half, came[:, :1024]])
    bt_near = jnp.stack([pick(bt_for, x, 1), came[:, 1024:].reshape(8, 4, 128).transpose(1, 0, 2)], axis=1)
    along_y = [
        over_y(jnp.concatenate([a_near, pick(bt_near, (y + k) % 4, 0)], axis=2), k) for k in (1, 2, 3)
    ]
    weight = frozen_projection_weight.reshape(16, 128, 1024)
    weight, grad_a, grad_bt, a_near = lax.optimization_barrier((weight, grad_a, grad_bt, a_near))
    arrived = lax.all_to_all(weight, "col", 0, 0, tiled=True)
    part = jnp.stack([a_near] + [came[:, :, :1024] for came in along_y])
    bt_rows = jnp.stack([pick(bt_near, y, 0)] + [came[:, :, 1024:] for came in along_y])
    part = hold(part.reshape(64, 1024)).reshape(4, 2, 8, 1024)
    part = jnp.stack([part, over_x_hi_x(part)[:, ::-1]], axis=2).reshape(4, 2, 16, 1024)
    a_parts = [part] + [over_z(part, k) for k in (1, 2, 3)]
    a_parts = a_parts + [over_core(part) for part in a_parts]
    saved = merge(bt_rows.reshape(R, 128).astype(jnp.float32), a_parts, arrived)
    a_new, a_first_new, a_second_new = adam_step(a_master, a_first, a_second, grad_a)
    bt_new, bt_first_new, bt_second_new = adam_step(bt_master, bt_first, bt_second, grad_bt)
    return (saved, a_new, a_first_new, a_second_new, bt_new, bt_first_new, bt_second_new)


def solution(mesh):
    return jax.shard_map(
        per_device,
        mesh=mesh,
        in_specs=(
            P("row", "col"),
            P("row", "col"),
            P("row", "col"),
            P("row", "col"),
            P("col", "row"),
            P("col", "row"),
            P("col", "row"),
            P("row", None, "col"),
            P("col", None, "row"),
        ),
        out_specs=(
            P(None, ("row", "col"), None),
            P("row", "col"),
            P("row", "col"),
            P("row", "col"),
            P("col", "row"),
            P("col", "row"),
            P("col", "row"),
        ),
        check_vma=False,
    )
```

```python
import math

import jax
import jax.numpy as jnp
from jax import lax
from jax.experimental import pallas as pl
from jax.experimental.pallas import tpu as pltpu
from jax.sharding import PartitionSpec as P

D = 16384
R = 64
TP = 8
STEP = 10


beta_first = 0.9
beta_second = 0.95
adam_eps = 1e-08
learn_rate = 0.08


def adapter_factor():
    return 0.25 / math.sqrt(R * D)


def adam_step(master, first, second, grad):
    first_new = beta_first * first + (1.0 - beta_first) * grad
    second_new = beta_second * second + (1.0 - beta_second) * grad * grad
    corr_first = 1.0 - beta_first**STEP
    corr_second = 1.0 - beta_second**STEP
    update = first_new / corr_first / (jnp.sqrt(second_new / corr_second) + adam_eps)
    return (master - learn_rate * update, first_new, second_new)


def mod4(value):
    return lax.rem(value + 4, 4)


def rank_order(y, x, core, x_hi, z):
    p = lax.broadcasted_iota(jnp.int32, (R, R), 0)
    s = lax.broadcasted_iota(jnp.int32, (R, R), 1)
    from_z = (z - p // 16 + 4) % 4
    from_x_hi = x_hi ^ ((p // 8) % 2)
    rank_a = 8 * (from_x_hi * 4 + from_z) + p % 8
    from_y = (y - s // 16 + 4) % 4
    from_x = x ^ ((s // 8) % 2)
    from_core = core ^ ((s // 4) % 2)
    rank_b = 4 * (from_y * 4 + from_x * 2 + from_core) + s % 4
    return (rank_a == rank_b).astype(jnp.bfloat16)


def reorder_kernel(bt_ref, left_ref):
    row, col = lax.axis_index("row"), lax.axis_index("col")
    x_hi, z = row // 4, row % 4
    y, x, core = col // 4, (col // 2) % 2, col % 2
    left_ref[...] = lax.dot_general(
        bt_ref[...].astype(jnp.bfloat16),
        rank_order(y, x, core, x_hi, z),
        (((0,), (1,)), ((), ())),
        preferred_element_type=jnp.float32,
    ).astype(jnp.bfloat16)


def reorder(bt_rows):
    return pl.pallas_call(reorder_kernel, out_shape=jax.ShapeDtypeStruct((128, R), jnp.bfloat16))(bt_rows)


def merge_kernel(left_ref, *refs):
    a_refs, arrived_ref, saved_ref = refs[:8], refs[8], refs[9]
    a_buf, in_buf, out_buf, a_sem, in_sem, out_sem = refs[10:]
    col = lax.axis_index("col")
    y, x, core = col // 4, (col // 2) % 2, col % 2

    def source(step):
        k_core, k_y, k_x = step // 8, (step // 2) % 4, step % 2
        return mod4(y - k_y) * 4 + (x ^ k_x) * 2 + (core ^ k_core)

    a_copies = [pltpu.make_async_copy(a_refs[i], a_buf.at[i], a_sem.at[i]) for i in range(8)]
    in_copies = [
        pltpu.make_async_copy(arrived_ref.at[source(s)], in_buf.at[s], in_sem.at[s])
        for s in range(16)
    ]
    out_copies = [
        pltpu.make_async_copy(
            out_buf.at[s],
            saved_ref.at[source(s) // 2, :, pl.ds((source(s) % 2) * 1024, 1024)],
            out_sem.at[s],
        )
        for s in range(16)
    ]
    for copy in a_copies[:4] + in_copies[:8] + a_copies[4:] + in_copies[8:]:
        copy.start()
    left = left_ref[...]
    for copy in a_copies:
        copy.wait()
    for first in range(0, 16, 4):
        group = range(first, first + 4)
        for s in group:
            in_copies[s].wait()
        for s in group:
            k_core, k_y, k_x = s // 8, (s // 2) % 4, s % 2
            a_block = jnp.concatenate(
                [a_buf[4 * k_core + k_z, k_y, k_x] for k_z in range(4)], axis=0
            )
            increment = lax.dot_general(
                left, a_block, (((1,), (0,)), ((), ())), preferred_element_type=jnp.float32
            )
            merged = in_buf[s].astype(jnp.float32) + adapter_factor() * increment
            out_buf[s] = merged.astype(jnp.bfloat16)
        for s in group:
            out_copies[s].start()
    for copy in out_copies:
        copy.wait()


def merge(left, a_parts, arrived):
    return pl.pallas_call(
        merge_kernel,
        in_specs=[pl.BlockSpec(memory_space=pltpu.VMEM)] + [pl.BlockSpec(memory_space=pl.ANY)] * 9,
        out_specs=pl.BlockSpec(memory_space=pl.ANY),
        out_shape=jax.ShapeDtypeStruct((8, 128, 2048), jnp.bfloat16),
        scratch_shapes=[
            pltpu.VMEM((8, 4, 2, 16, 1024), jnp.bfloat16),
            pltpu.VMEM((16, 128, 1024), jnp.bfloat16),
            pltpu.VMEM((16, 128, 1024), jnp.bfloat16),
            pltpu.SemaphoreType.DMA((8,)),
            pltpu.SemaphoreType.DMA((16,)),
            pltpu.SemaphoreType.DMA((16,)),
        ],
        compiler_params=pltpu.CompilerParams(vmem_limit_bytes=16 << 20),
        cost_estimate=pl.CostEstimate(
            flops=2 * 128 * 64 * 16384, bytes_accessed=10 << 20, transcendentals=0
        ),
    )(left, *a_parts, arrived)


def hold_kernel(array_ref, held_ref):
    held_ref[...] = array_ref[...]


def hold(array):
    return pl.pallas_call(
        hold_kernel,
        out_shape=jax.ShapeDtypeStruct(array.shape, array.dtype),
        cost_estimate=pl.CostEstimate(flops=100000000000, bytes_accessed=1 << 18, transcendentals=0),
    )(array)


def pick(array, index, axis):
    return lax.dynamic_index_in_dim(array, index, axis, keepdims=False)


def over_core(array):
    return lax.ppermute(array, "col", [(i, i ^ 1) for i in range(16)])


def over_x(array):
    return lax.ppermute(array, "col", [(i, i ^ 2) for i in range(16)])


def over_y(array, k):
    return lax.ppermute(array, "col", [(i, (i + 4 * k) % 16) for i in range(16)])


def over_x_y(array, k_x, k_y):
    return lax.ppermute(array, "col", [(i, ((i + 4 * k_y) % 16) ^ (2 * k_x)) for i in range(16)])


def over_col(array, mask):
    return lax.ppermute(array, "col", [(i, i ^ mask) for i in range(16)])


def over_row(array, mask):
    return lax.ppermute(array, "row", [(i, i ^ mask) for i in range(8)])


def two_of(array, first, second, axis):
    return jnp.stack([pick(array, first, axis), pick(array, second, axis)], axis=axis)


def over_x_hi(array):
    return lax.ppermute(array, "row", [(i, i ^ 4) for i in range(8)])


def over_x_hi_x(array):
    return lax.ppermute(array, ("row", "col"), [(i, i ^ (4 * 16 + 2)) for i in range(128)])


def over_z(array, k):
    return lax.ppermute(array, "row", [(i, i // 4 * 4 + (i + k) % 4) for i in range(8)])


def per_device(
    frozen_projection_weight,
    a_master,
    a_first,
    a_second,
    bt_master,
    bt_first,
    bt_second,
    grad_a_parts,
    grad_bt_parts,
):
    row, col = lax.axis_index("row"), lax.axis_index("col")
    x_hi, z = row // 4, row % 4
    y, x, core = col // 4, (col // 2) % 2, col % 2

    bt_part = grad_bt_parts.reshape(4, 2, 2, 4, 2048)
    kept, sent = lax.optimization_barrier((pick(bt_part, core, 2), pick(bt_part, 1 - core, 2)))
    bt_part = kept + over_core(sent)
    part = grad_a_parts.reshape(2, 4, 8, 1024)
    kept, *sent = lax.optimization_barrier([pick(part, (z + k) % 4, 1) for k in range(4)])
    bt_part, *sent = lax.optimization_barrier((bt_part, *sent))
    part = kept + sum(over_z(sent[k - 1], k) for k in (3, 2, 1))
    grad_a = pick(part, x_hi, 0) + over_x_hi(pick(part, 1 - x_hi, 0))
    bt_part = two_of(bt_part, y, y ^ 1, 0) + over_col(two_of(bt_part, y ^ 3, y ^ 2, 0), 12)
    bt_part = bt_part[0] + over_col(bt_part[1], 4)
    grad_bt = pick(bt_part, x, 0) + over_x(pick(bt_part, 1 - x, 0))

    a_new = adam_step(a_master, a_first, a_second, grad_a)[0]
    bt_new = adam_step(bt_master, bt_first, bt_second, grad_bt)[0]

    part = bt_new.reshape(4, 4, 2, 2, 128).transpose(1, 2, 3, 0, 4)
    part = jnp.concatenate([pick(part, core, 2), over_core(pick(part, 1 - core, 2))], axis=2)
    bt_for = part.astype(jnp.bfloat16)
    a_half = a_new.astype(jnp.bfloat16)
    sent = pick(bt_for, 1 - x, 1).transpose(1, 0, 2).reshape(8, 512)
    came = over_x(jnp.concatenate([a_half, sent], axis=1))
    a_near = jnp.stack([a_half, came[:, :1024]])
    bt_near = jnp.stack([pick(bt_for, x, 1), came[:, 1024:].reshape(8, 4, 128).transpose(1, 0, 2)], axis=1)
    along_y = [
        over_y(jnp.concatenate([a_near, pick(bt_near, (y + k) % 4, 0)], axis=2), k) for k in (1, 2, 3)
    ]
    weight = frozen_projection_weight.reshape(16, 128, 1024)
    weight, grad_a, grad_bt, a_near = lax.optimization_barrier((weight, grad_a, grad_bt, a_near))
    arrived = lax.all_to_all(weight, "col", 0, 0, tiled=True)
    part = jnp.stack([a_near] + [came[:, :, :1024] for came in along_y])
    bt_rows = jnp.stack([pick(bt_near, y, 0)] + [came[:, :, 1024:] for came in along_y])
    part = hold(part.reshape(64, 1024)).reshape(4, 2, 8, 1024)
    part = jnp.stack([part, over_x_hi_x(part)[:, ::-1]], axis=2).reshape(4, 2, 16, 1024)
    a_parts = [part] + [over_z(part, k) for k in (1, 2, 3)]
    a_parts = a_parts + [over_core(part) for part in a_parts]
    saved = merge(reorder(bt_rows.reshape(R, 128).astype(jnp.float32)), a_parts, arrived)
    a_new, a_first_new, a_second_new = adam_step(a_master, a_first, a_second, grad_a)
    bt_new, bt_first_new, bt_second_new = adam_step(bt_master, bt_first, bt_second, grad_bt)
    return (saved, a_new, a_first_new, a_second_new, bt_new, bt_first_new, bt_second_new)


def solution(mesh):
    return jax.shard_map(
        per_device,
        mesh=mesh,
        in_specs=(
            P("row", "col"),
            P("row", "col"),
            P("row", "col"),
            P("row", "col"),
            P("col", "row"),
            P("col", "row"),
            P("col", "row"),
            P("row", None, "col"),
            P("col", None, "row"),
        ),
        out_specs=(
            P(None, ("row", "col"), None),
            P("row", "col"),
            P("row", "col"),
            P("row", "col"),
            P("col", "row"),
            P("col", "row"),
            P("col", "row"),
        ),
        check_vma=False,
    )
```

```python
import math

import jax
import jax.numpy as jnp
from jax import lax
from jax.experimental import pallas as pl
from jax.experimental.pallas import tpu as pltpu
from jax.sharding import PartitionSpec as P

D = 16384
R = 64
TP = 8
STEP = 10


beta_first = 0.9
beta_second = 0.95
adam_eps = 1e-08
learn_rate = 0.08


def adapter_factor():
    return 0.25 / math.sqrt(R * D)


def adam_step(master, first, second, grad):
    first_new = beta_first * first + (1.0 - beta_first) * grad
    second_new = beta_second * second + (1.0 - beta_second) * grad * grad
    corr_first = 1.0 - beta_first**STEP
    corr_second = 1.0 - beta_second**STEP
    update = first_new / corr_first / (jnp.sqrt(second_new / corr_second) + adam_eps)
    return (master - learn_rate * update, first_new, second_new)


def mod4(value):
    return lax.rem(value + 4, 4)


def rank_order(y, x, core, x_hi, z):
    p = lax.broadcasted_iota(jnp.int32, (R, R), 0)
    s = lax.broadcasted_iota(jnp.int32, (R, R), 1)
    from_z = (z - p // 16 + 4) % 4
    from_x_hi = x_hi ^ ((p // 8) % 2)
    rank_a = 8 * (from_x_hi * 4 + from_z) + p % 8
    from_y = (y - s // 16 + 4) % 4
    from_x = x ^ ((s // 8) % 2)
    from_core = core ^ ((s // 4) % 2)
    rank_b = 4 * (from_y * 4 + from_x * 2 + from_core) + s % 4
    return (rank_a == rank_b).astype(jnp.bfloat16)


def merge_kernel(bt_ref, *refs):
    a_refs, arrived_ref, saved_ref = refs[:8], refs[8], refs[9]
    a_buf, in_buf, out_buf, a_sem, in_sem, out_sem = refs[10:]
    row, col = lax.axis_index("row"), lax.axis_index("col")
    x_hi, z = row // 4, row % 4
    y, x, core = col // 4, (col // 2) % 2, col % 2

    def source(step):
        k_core, k_y, k_x = step // 8, (step // 2) % 4, step % 2
        return mod4(y - k_y) * 4 + (x ^ k_x) * 2 + (core ^ k_core)

    a_copies = [pltpu.make_async_copy(a_refs[i], a_buf.at[i], a_sem.at[i]) for i in range(8)]
    in_copies = [
        pltpu.make_async_copy(arrived_ref.at[source(s)], in_buf.at[s], in_sem.at[s])
        for s in range(16)
    ]
    out_copies = [
        pltpu.make_async_copy(
            out_buf.at[s],
            saved_ref.at[source(s) // 2, :, pl.ds((source(s) % 2) * 1024, 1024)],
            out_sem.at[s],
        )
        for s in range(16)
    ]
    for copy in a_copies[:4] + in_copies[:8] + a_copies[4:] + in_copies[8:]:
        copy.start()
    left = lax.dot_general(
        bt_ref[...].astype(jnp.bfloat16),
        rank_order(y, x, core, x_hi, z),
        (((0,), (1,)), ((), ())),
        preferred_element_type=jnp.float32,
    ).astype(jnp.bfloat16)
    for copy in a_copies:
        copy.wait()
    for first, last in ((0, 2), (2, 6), (6, 10), (10, 14), (14, 16)):
        group = range(first, last)
        for s in group:
            in_copies[s].wait()
        for s in group:
            k_core, k_y, k_x = s // 8, (s // 2) % 4, s % 2
            a_block = jnp.concatenate(
                [a_buf[4 * k_core + k_z, k_y, k_x] for k_z in range(4)], axis=0
            )
            increment = lax.dot_general(
                left, a_block, (((1,), (0,)), ((), ())), preferred_element_type=jnp.float32
            )
            merged = in_buf[s].astype(jnp.float32) + adapter_factor() * increment
            out_buf[s] = merged.astype(jnp.bfloat16)
        for s in group:
            out_copies[s].start()
    for copy in out_copies:
        copy.wait()


def merge(bt_rows, a_parts, arrived):
    return pl.pallas_call(
        merge_kernel,
        in_specs=[pl.BlockSpec(memory_space=pltpu.VMEM)] + [pl.BlockSpec(memory_space=pl.ANY)] * 9,
        out_specs=pl.BlockSpec(memory_space=pl.ANY),
        out_shape=jax.ShapeDtypeStruct((8, 128, 2048), jnp.bfloat16),
        scratch_shapes=[
            pltpu.VMEM((8, 4, 2, 16, 1024), jnp.bfloat16),
            pltpu.VMEM((16, 128, 1024), jnp.bfloat16),
            pltpu.VMEM((16, 128, 1024), jnp.bfloat16),
            pltpu.SemaphoreType.DMA((8,)),
            pltpu.SemaphoreType.DMA((16,)),
            pltpu.SemaphoreType.DMA((16,)),
        ],
        compiler_params=pltpu.CompilerParams(vmem_limit_bytes=16 << 20),
        cost_estimate=pl.CostEstimate(
            flops=2 * 128 * 64 * 16384, bytes_accessed=10 << 20, transcendentals=0
        ),
    )(bt_rows, *a_parts, arrived)


def hold_kernel(array_ref, held_ref):
    held_ref[...] = array_ref[...]


def hold(array):
    return pl.pallas_call(
        hold_kernel,
        out_shape=jax.ShapeDtypeStruct(array.shape, array.dtype),
        cost_estimate=pl.CostEstimate(flops=100000000000, bytes_accessed=1 << 18, transcendentals=0),
    )(array)


def pick(array, index, axis):
    return lax.dynamic_index_in_dim(array, index, axis, keepdims=False)


def over_core(array):
    return lax.ppermute(array, "col", [(i, i ^ 1) for i in range(16)])


def over_x(array):
    return lax.ppermute(array, "col", [(i, i ^ 2) for i in range(16)])


def over_y(array, k):
    return lax.ppermute(array, "col", [(i, (i + 4 * k) % 16) for i in range(16)])


def over_x_y(array, k_x, k_y):
    return lax.ppermute(array, "col", [(i, ((i + 4 * k_y) % 16) ^ (2 * k_x)) for i in range(16)])


def over_col(array, mask):
    return lax.ppermute(array, "col", [(i, i ^ mask) for i in range(16)])


def over_row(array, mask):
    return lax.ppermute(array, "row", [(i, i ^ mask) for i in range(8)])


def two_of(array, first, second, axis):
    return jnp.stack([pick(array, first, axis), pick(array, second, axis)], axis=axis)


def over_x_hi(array):
    return lax.ppermute(array, "row", [(i, i ^ 4) for i in range(8)])


def over_x_hi_x(array):
    return lax.ppermute(array, ("row", "col"), [(i, i ^ (4 * 16 + 2)) for i in range(128)])


def over_z(array, k):
    return lax.ppermute(array, "row", [(i, i // 4 * 4 + (i + k) % 4) for i in range(8)])


def per_device(
    frozen_projection_weight,
    a_master,
    a_first,
    a_second,
    bt_master,
    bt_first,
    bt_second,
    grad_a_parts,
    grad_bt_parts,
):
    row, col = lax.axis_index("row"), lax.axis_index("col")
    x_hi, z = row // 4, row % 4
    y, x, core = col // 4, (col // 2) % 2, col % 2

    bt_part = grad_bt_parts.reshape(4, 2, 2, 4, 2048)
    kept, sent = lax.optimization_barrier((pick(bt_part, core, 2), pick(bt_part, 1 - core, 2)))
    bt_part = kept + over_core(sent)
    part = grad_a_parts.reshape(2, 4, 8, 1024)
    kept, *sent = lax.optimization_barrier([pick(part, (z + k) % 4, 1) for k in range(4)])
    bt_part, *sent = lax.optimization_barrier((bt_part, *sent))
    part = kept + sum(over_z(sent[k - 1], k) for k in (3, 2, 1))
    grad_a = pick(part, x_hi, 0) + over_x_hi(pick(part, 1 - x_hi, 0))
    bt_part = two_of(bt_part, y, y ^ 1, 0) + over_col(two_of(bt_part, y ^ 3, y ^ 2, 0), 12)
    bt_part = bt_part[0] + over_col(bt_part[1], 4)
    grad_bt = pick(bt_part, x, 0) + over_x(pick(bt_part, 1 - x, 0))

    a_new = adam_step(a_master, a_first, a_second, grad_a)[0]
    bt_new = adam_step(bt_master, bt_first, bt_second, grad_bt)[0]

    part = bt_new.reshape(4, 4, 2, 2, 128).transpose(1, 2, 3, 0, 4)
    part = jnp.concatenate([pick(part, core, 2), over_core(pick(part, 1 - core, 2))], axis=2)
    bt_for = part.astype(jnp.bfloat16)
    a_half = a_new.astype(jnp.bfloat16)
    sent = pick(bt_for, 1 - x, 1).transpose(1, 0, 2).reshape(8, 512)
    came = over_x(jnp.concatenate([a_half, sent], axis=1))
    a_near = jnp.stack([a_half, came[:, :1024]])
    bt_near = jnp.stack([pick(bt_for, x, 1), came[:, 1024:].reshape(8, 4, 128).transpose(1, 0, 2)], axis=1)
    along_y = [
        over_y(jnp.concatenate([a_near, pick(bt_near, (y + k) % 4, 0)], axis=2), k) for k in (1, 2, 3)
    ]
    weight = frozen_projection_weight.reshape(16, 128, 1024)
    weight, grad_a, grad_bt, a_near = lax.optimization_barrier((weight, grad_a, grad_bt, a_near))
    arrived = lax.all_to_all(weight, "col", 0, 0, tiled=True)
    part = jnp.stack([a_near] + [came[:, :, :1024] for came in along_y])
    bt_rows = jnp.stack([pick(bt_near, y, 0)] + [came[:, :, 1024:] for came in along_y])
    part = hold(part.reshape(64, 1024)).reshape(4, 2, 8, 1024)
    part = jnp.stack([part, over_x_hi_x(part)[:, ::-1]], axis=2).reshape(4, 2, 16, 1024)
    a_parts = [part] + [over_z(part, k) for k in (1, 2, 3)]
    a_parts = a_parts + [over_core(part) for part in a_parts]
    saved = merge(bt_rows.reshape(R, 128).astype(jnp.float32), a_parts, arrived)
    a_new, a_first_new, a_second_new = adam_step(a_master, a_first, a_second, grad_a)
    bt_new, bt_first_new, bt_second_new = adam_step(bt_master, bt_first, bt_second, grad_bt)
    return (saved, a_new, a_first_new, a_second_new, bt_new, bt_first_new, bt_second_new)


def solution(mesh):
    return jax.shard_map(
        per_device,
        mesh=mesh,
        in_specs=(
            P("row", "col"),
            P("row", "col"),
            P("row", "col"),
            P("row", "col"),
            P("col", "row"),
            P("col", "row"),
            P("col", "row"),
            P("row", None, "col"),
            P("col", None, "row"),
        ),
        out_specs=(
            P(None, ("row", "col"), None),
            P("row", "col"),
            P("row", "col"),
            P("row", "col"),
            P("col", "row"),
            P("col", "row"),
            P("col", "row"),
        ),
        check_vma=False,
    )
```
